512 devices in a mesh: tm: 4 (over z_lo), row: 16 (over y, core), head: 8 (over x, z_hi).
Axes of the slice: x: 4, y: 8, z: 8 (z_hi: 2, z_lo: 4; z = z_hi * 4 + z_lo), core: 2. Of those that a mesh axis runs over, the one named last changes fastest.
Arguments:
- queries: bfloat16 [8, 64, 16, 5120], P('tm', 'row', None, 'head'), may hold values from -24 to 24
- key_states: bfloat16 [8, 64, 16, 5120], P('tm', 'row', None, 'head'), may hold values from -24 to 24
- value_states: bfloat16 [8, 64, 16, 5120], P('tm', 'row', None, 'head'), may hold values from -6 to 6
- grad_output: bfloat16 [8, 64, 16, 5120], P('tm', 'row', None, 'head'), may hold values from -6 to 6
- window_mask: int32 [4, 32, 1, 27], P('tm', 'row'), may hold values from 0 to 1, as said below
- row_valid: int32 [8, 64], replicated, may hold values 0 or 1
Outputs:
- output: bfloat16 [8, 64, 16, 5120], P('tm', 'row', None, 'head')
- grad_queries: bfloat16 [8, 64, 16, 5120], P('tm', 'row', None, 'head')
- grad_keys: bfloat16 [8, 64, 16, 5120], P('tm', 'row', None, 'head')
- grad_values: bfloat16 [8, 64, 16, 5120], P('tm', 'row', None, 'head')
The draws below stay inside these ranges and needn't reach their ends.
Inputs may be any that keep to these rules, and one draw needn't show every extreme that they name: `window_mask`: entry 13 (the tile itself) is 1 for every tile; entries whose tile lies outside the grid are 0; the mask is symmetric: tile A keeps tile B exactly when B keeps A at the opposite offset.
All inputs are finite; a program needn't handle non-finite values.
Results may differ from the reference program's by a relative error of at most 0.012.
Values may be sent and summed in bfloat16 or wider, within the bound.
No kernel may reach another device: no remote copies, remote signals or barrier semaphores. Data moves between devices by JAX's collectives and lax.ppermute only.
A program may use at most 64 MiB of HBM per device.

```python
import jax
import jax.numpy as jnp
from jax import lax

HD = 128
HEADS = 40
TF = 2
TR = 2
TC = 16
NF = 8
NR = 64
W = 16


def draw_queries(key, part):
    key = jax.random.fold_in(key, 1)
    field_shape = (NF, NR, W, HEADS * HD)
    return jnp.clip(jax.random.normal(key, field_shape, jnp.float32), -4.0, 4.0).astype(jnp.bfloat16)


def draw_key_states(key, part):
    key = jax.random.fold_in(key, 2)
    field_shape = (NF, NR, W, HEADS * HD)
    return jnp.clip(jax.random.normal(key, field_shape, jnp.float32), -4.0, 4.0).astype(jnp.bfloat16)


def draw_window_mask(key, part):
    key = jax.random.fold_in(key, 11)
    frame_tiles = NF // TF
    row_tiles = NR // TR
    col_tiles = W // TC
    levels = jax.random.randint(key, (frame_tiles, row_tiles, col_tiles), 0, 6)
    padded = jnp.pad(levels, 1, constant_values=-100)
    columns = []
    for offset in range(27):
        frame_step = offset // 9
        row_step = offset // 3 % 3
        col_step = offset % 3
        nearby = padded[frame_step:frame_step + frame_tiles, row_step:row_step + row_tiles, col_step:col_step + col_tiles]
        kept_tiles = (levels + nearby >= 5).astype(jnp.int32)
        if offset == 13:
            kept_tiles = jnp.ones_like(levels)
        columns.append(kept_tiles)
    return jnp.stack(columns, axis=-1)


def plant(values, key, low, largest):
    extent = values.shape
    index_at = [jax.random.randint(jax.random.fold_in(key, axis), (), 0, extent[axis]) for axis in range(len(extent))]
    values = values.at[tuple(index_at)].set(low)
    longest = extent.index(max(extent))
    index_at[longest] = (index_at[longest] + 1) % extent[longest]
    return values.at[tuple(index_at)].set(largest)


def level_of(key, extent, cuts, least, largest):
    loudness = 1.0
    for dim, blocks in cuts:
        draws = jax.random.uniform(jax.random.fold_in(jax.random.fold_in(key, 6), dim), (blocks,), jnp.float32, least / len(cuts), largest / len(cuts))
        loudness = loudness * jnp.repeat(jnp.exp(draws), extent[dim] // blocks).reshape((-1,) + (1,) * (len(extent) - 1 - dim))
    return loudness


def normal_values(key, dims, scale, reach, split=(), held_as=jnp.bfloat16):
    entries = jax.random.normal(key, dims, jnp.float32) * scale
    if len(split) > 0:
        entries = level_of(key, dims, split, -0.22, 0.18) * entries
    return jnp.clip(entries, min=-reach, max=reach).astype(held_as)


def setup_inputs(seed: int = 0) -> dict:
    arg_keys = jax.random.split(jax.random.key(seed), 7)
    return {
        "queries": draw_queries(jax.random.fold_in(arg_keys[6], 71), 0),
        "key_states": draw_key_states(jax.random.fold_in(arg_keys[6], 71), 0),
        "value_states": normal_values(arg_keys[2], (NF, NR, W, HEADS * HD), 1.0, 6.0, ((0, 4), (1, 16), (3, 8))),
        "grad_output": normal_values(arg_keys[3], (NF, NR, W, HEADS * HD), 1.0, 6.0, ((0, 4), (1, 16), (3, 8))),
        "window_mask": draw_window_mask(jax.random.fold_in(arg_keys[6], 71), 0),
        "row_valid": plant((jax.random.randint(arg_keys[5], (NF, NR), 0, 8) < 7).astype(jnp.int32), jax.random.fold_in(arg_keys[5], 1), 0, 1),
    }


far_below = -1.0e30


def tile_pass(query_tile, key_block, value_block, grad_tile, keep, query_live):
    score_scale = HD ** -0.5
    allowed = query_live[:, None] & keep[None, :]
    scores = jnp.dot(query_tile, key_block.T, preferred_element_type=jnp.float32) * score_scale
    row_max = jnp.max(jnp.where(allowed, scores, far_below), axis=1, keepdims=True)
    unnormed = jnp.exp(jnp.where(allowed, scores - row_max, -jnp.inf))
    live_float = query_live.astype(jnp.float32)[:, None]
    denominator = jnp.sum(unnormed, axis=1, keepdims=True) + (1.0 - live_float)
    attended = jnp.dot(unnormed.astype(jnp.bfloat16), value_block, preferred_element_type=jnp.float32) / denominator
    tile_output = attended.astype(jnp.bfloat16)
    log_total = jnp.where(query_live[:, None], row_max + jnp.log(denominator), 0.0)
    row_dot = jnp.sum(tile_output.astype(jnp.float32) * grad_tile.astype(jnp.float32), axis=1, keepdims=True)
    weights = jnp.exp(jnp.where(allowed, scores - log_total, -jnp.inf))
    value_terms = jnp.dot(weights.astype(jnp.bfloat16).T, grad_tile, preferred_element_type=jnp.float32)
    grad_probs = jnp.dot(grad_tile, value_block.T, preferred_element_type=jnp.float32)
    grad_scores = (weights * (grad_probs - row_dot)).astype(jnp.bfloat16)
    query_terms = (jnp.dot(grad_scores, key_block, preferred_element_type=jnp.float32) * score_scale).astype(jnp.bfloat16)
    key_terms = jnp.dot(grad_scores.T, query_tile, preferred_element_type=jnp.float32) * score_scale
    return tile_output, query_terms, key_terms, value_terms


def one_head(queries, key_states, value_states, grad_output, window_mask, row_valid, head_index):
    start = head_index * HD
    query_head = lax.dynamic_slice_in_dim(queries, start, HD, 3)
    key_head = lax.dynamic_slice_in_dim(key_states, start, HD, 3)
    value_head = lax.dynamic_slice_in_dim(value_states, start, HD, 3)
    grad_head = lax.dynamic_slice_in_dim(grad_output, start, HD, 3)
    pad_spec = ((TF, TF), (TR, TR), (TC, TC), (0, 0))
    key_pad = jnp.pad(key_head, pad_spec)
    value_pad = jnp.pad(value_head, pad_spec)
    valid_pad = jnp.pad(row_valid, ((TF, TF), (TR, TR)))
    row_tiles = NR // TR
    col_tiles = W // TC
    tile_count = (NF // TF) * row_tiles * col_tiles
    anchor = jnp.zeros((), jnp.int32)
    region_shape = (3 * TF, 3 * TR, 3 * TC, HD)

    def visit(carry, tile_index):
        output_grid, query_grads, key_grads, value_grads = carry
        frame_first = (tile_index // (row_tiles * col_tiles)) * TF
        row_first = ((tile_index // col_tiles) % row_tiles) * TR
        col_first = (tile_index % col_tiles) * TC
        corner = (frame_first, row_first, col_first, anchor)
        query_tile = lax.dynamic_slice(query_head, corner, (TF, TR, TC, HD)).reshape(-1, HD)
        grad_tile = lax.dynamic_slice(grad_head, corner, (TF, TR, TC, HD)).reshape(-1, HD)
        key_block = lax.dynamic_slice(key_pad, corner, region_shape).reshape(-1, HD)
        value_block = lax.dynamic_slice(value_pad, corner, region_shape).reshape(-1, HD)
        tile_keep = lax.dynamic_slice(window_mask, (frame_first // TF, row_first // TR, col_first // TC, anchor), (1, 1, 1, 27)).reshape(3, 3, 3)
        grown = jnp.repeat(jnp.repeat(jnp.repeat(tile_keep, TF, 0), TR, 1), TC, 2)
        near_valid = lax.dynamic_slice(valid_pad, (frame_first, row_first), (3 * TF, 3 * TR))
        keep = ((grown > 0) & (near_valid[:, :, None] > 0)).reshape(-1)
        own_valid = lax.dynamic_slice(row_valid, (frame_first, row_first), (TF, TR)) > 0
        query_live = jnp.broadcast_to(own_valid[:, :, None], (TF, TR, TC)).reshape(-1)
        tile_output, query_terms, key_terms, value_terms = tile_pass(query_tile, key_block, value_block, grad_tile, keep, query_live)
        output_grid = lax.dynamic_update_slice(output_grid, tile_output.reshape(TF, TR, TC, HD), corner)
        query_grads = lax.dynamic_update_slice(query_grads, query_terms.reshape(TF, TR, TC, HD), corner)
        old_keys = lax.dynamic_slice(key_grads, corner, region_shape)
        key_grads = lax.dynamic_update_slice(key_grads, old_keys + key_terms.reshape(region_shape), corner)
        old_values = lax.dynamic_slice(value_grads, corner, region_shape)
        value_grads = lax.dynamic_update_slice(value_grads, old_values + value_terms.reshape(region_shape), corner)
        return (output_grid, query_grads, key_grads, value_grads), None

    start_carry = (jnp.zeros((NF, NR, W, HD), jnp.bfloat16), jnp.zeros((NF, NR, W, HD), jnp.bfloat16), jnp.zeros(key_pad.shape, jnp.float32), jnp.zeros(value_pad.shape, jnp.float32))
    final, unused = lax.scan(visit, start_carry, jnp.arange(tile_count, dtype=jnp.int32))
    output_grid, query_grads, key_grads, value_grads = final
    key_out = key_grads[TF:TF + NF, TR:TR + NR, TC:TC + W].astype(jnp.bfloat16)
    value_out = value_grads[TF:TF + NF, TR:TR + NR, TC:TC + W].astype(jnp.bfloat16)
    return output_grid, query_grads, key_out, value_out


def reference(queries, key_states, value_states, grad_output, window_mask, row_valid):
    def per_head(head_index):
        return one_head(queries, key_states, value_states, grad_output, window_mask, row_valid, head_index)

    results = lax.map(per_head, jnp.arange(HEADS, dtype=jnp.int32))
    merged = tuple(jnp.moveaxis(stacked_heads, 0, 3).reshape(NF, NR, W, HEADS * HD) for stacked_heads in results)
    return merged[0], merged[1], merged[2], merged[3]
```

```python
import functools
import math

import jax
import jax.numpy as jnp
import numpy as np
from jax import lax
from jax.experimental import pallas as pl
from jax.experimental.pallas import tpu as pltpu
from jax.sharding import PartitionSpec as P

HD = 128
TF = 2
TR = 2
BAND = 64
HALF = BAND // 2
NEAR = 3 * TF * BAND
Q_AT = 2 * NEAR
G_AT = Q_AT + TF * BAND
MASK_AT = G_AT + TF * BAND
MASK_ROWS = 16
MESSAGE = MASK_AT + MASK_ROWS
OWN = TF * BAND
GROUPS = ((0, 5),)

SCALE = HD ** (-0.5)
SCALE_LOG2 = SCALE * math.log2(math.e)
FAR = 1e30


def contract(left, right, dims):
    return lax.dot_general(left, right, ((dims[:1], dims[1:]), ((), ())), preferred_element_type=jnp.float32)


SLOT_TILE = (2, 3, 1, 4)


def other_tile(slot, half):
    return ((1, 4), (1, 4), (0, 1), (4, 5))[slot][half]


def selectors():
    mask_pick = np.zeros((128, 2 * NEAR), np.float32)
    valid_pick = np.zeros((128, 4 * NEAR), np.float32)
    query_pick = np.zeros((4 * BAND, 128), np.float32)
    for lane in range(NEAR):
        frame, half, row = lane // BAND, lane % BAND // HALF, lane % HALF // 16
        valid_pick[frame * 12 + 4 + 2 * half + row, lane] = 1
        for part, slot in enumerate((0, 2, 3)):
            valid_pick[frame * 12 + 2 * other_tile(slot, half) + row, (part + 1) * NEAR + lane] = 1
        for slot in range(4):
            for part, tile in enumerate((2 + half, other_tile(slot, half))):
                step = tile - SLOT_TILE[slot]
                if abs(step) <= 1:
                    mask_pick[32 * slot + 9 * (frame // TF) + 3 * (step + 1) + 1, part * NEAR + lane] = 1
    for slot in range(4):
        for token in range(BAND):
            frame, row = token // HALF, token % HALF // 16
            query_pick[slot * BAND + token, (TF + frame) * 12 + 2 * SLOT_TILE[slot] + row] = 1
    return mask_pick, valid_pick, query_pick


def tiles(here, above, below, at, lanes):
    def piece(ref, frame, half):
        start = at + frame * BAND + half * HALF
        return ref[start : start + HALF, lanes]

    order = ((here, 0), (here, 1), (above, 1), (below, 0))
    return jnp.concatenate([piece(ref, frame, half) for ref, half in order for frame in range(TF)], axis=0)


def beside(above, below, at, lanes):
    parts = []
    for frame in range(3 * TF):
        start = at + frame * BAND
        parts += [above[start + HALF : start + BAND, lanes], below[start : start + HALF, lanes]]
    return jnp.concatenate(parts, axis=0)


def store_tiles(ref, value, lanes):
    for half in range(2):
        for frame in range(TF):
            start = frame * BAND + half * HALF
            source = half * BAND + frame * HALF
            ref[start : start + HALF, lanes] = value[source : source + HALF]


def attend(
    heads, here, above, below, valid, mask_pick, valid_pick, query_pick, output, grad_query, own_sum, low_sum, high_sum
):
    mask_lanes = slice(MASK_AT, MASK_AT + MASK_ROWS)
    slot = lax.broadcasted_iota(jnp.int32, (MASK_ROWS, 128), 0)
    masks = jnp.where(
        slot < 2,
        here[mask_lanes, :128].astype(jnp.float32),
        jnp.where(slot == 2, above[mask_lanes, :128].astype(jnp.float32), below[mask_lanes, :128].astype(jnp.float32)),
    ).astype(jnp.bfloat16)
    kept = contract(masks, mask_pick[...], (1, 0))
    live = contract(valid[...], valid_pick[...], (1, 0))
    query_live = contract(query_pick[...], valid[...], (1, 1))[:, :1]
    bias_own, bias_other = [], []
    for index in range(4):
        part = max(index - 1, 0) + 1
        keep_own = kept[index : index + 1, :NEAR] * live[:1, :NEAR]
        keep_other = kept[index : index + 1, NEAR:] * live[:1, part * NEAR : (part + 1) * NEAR]
        bias_own.append(jnp.broadcast_to((keep_own - 1.0) * FAR, (BAND, NEAR)))
        bias_other.append(jnp.broadcast_to((keep_other - 1.0) * FAR, (BAND, NEAR)))
    bias_own = jnp.concatenate(bias_own, axis=0)
    bias_other = jnp.concatenate(bias_other, axis=0)

    for head in range(heads):
        lanes = slice(head * HD, (head + 1) * HD)
        query = tiles(here, above, below, Q_AT, lanes)
        grad = tiles(here, above, below, G_AT, lanes)
        key_own, value_own = here[:NEAR, lanes], here[NEAR : 2 * NEAR, lanes]
        key_up, value_up = above[:NEAR, lanes], above[NEAR : 2 * NEAR, lanes]
        key_down, value_down = below[:NEAR, lanes], below[NEAR : 2 * NEAR, lanes]
        key_side, value_side = beside(above, below, 0, lanes), beside(above, below, NEAR, lanes)

        score_own = contract(query, key_own, (1, 1)) * SCALE_LOG2 + bias_own
        score_other = (
            jnp.concatenate(
                [
                    contract(query[:OWN], key_side, (1, 1)),
                    contract(query[OWN : OWN + BAND], key_up, (1, 1)),
                    contract(query[OWN + BAND :], key_down, (1, 1)),
                ],
                axis=0,
            )
            * SCALE_LOG2
            + bias_other
        )
        row_max = jnp.max(jnp.maximum(score_own, score_other), axis=1, keepdims=True)
        own = jnp.exp2(score_own - row_max)
        other = jnp.exp2(score_other - row_max)
        share = query_live / jnp.sum(own + other, axis=1, keepdims=True)
        own_bf, other_bf = own.astype(jnp.bfloat16), other.astype(jnp.bfloat16)
        attended = contract(own_bf, value_own, (1, 0)) + jnp.concatenate(
            [
                contract(other_bf[:OWN], value_side, (1, 0)),
                contract(other_bf[OWN : OWN + BAND], value_up, (1, 0)),
                contract(other_bf[OWN + BAND :], value_down, (1, 0)),
            ],
            axis=0,
        )
        result = (attended * share).astype(jnp.bfloat16)
        row_dot = jnp.sum(result.astype(jnp.float32) * grad.astype(jnp.float32), axis=1, keepdims=True)
        weight_own = own * share
        weight_side = other[:OWN] * share[:OWN]
        grad_score_own = (weight_own * (contract(grad, value_own, (1, 1)) - row_dot)).astype(jnp.bfloat16)
        grad_score_side = (weight_side * (contract(grad[:OWN], value_side, (1, 1)) - row_dot[:OWN])).astype(jnp.bfloat16)
        query_sum = contract(grad_score_own[:OWN], key_own, (1, 0)) + contract(grad_score_side, key_side, (1, 0))
        key_sum = contract(grad_score_own, query, (0, 0)) * SCALE
        value_sum = contract(weight_own.astype(jnp.bfloat16), grad, (0, 0))

        store_tiles(output, result, lanes)
        store_tiles(grad_query, (query_sum * SCALE).astype(jnp.bfloat16), lanes)
        for part, total in enumerate((key_sum, value_sum)):
            rows = slice(part * OWN, (part + 1) * OWN)
            low_sum[rows, lanes] = total[:OWN].astype(jnp.bfloat16)
            own_sum[rows, lanes] = total[OWN : 2 * OWN]
            high_sum[rows, lanes] = total[2 * OWN :].astype(jnp.bfloat16)


def shifted(value, axis, steps):
    count = lax.axis_size(axis)
    leading, last = (max(0, -steps), min(count, count - steps))
    return lax.ppermute(value, axis, [(source, source + steps) for source in range(leading, last)])


def mask_block(window_mask, width):
    upper, lower = (window_mask[0, tile, 0].astype(jnp.bfloat16) for tile in range(2))
    rows = [jnp.pad(row, (32 * slot, width - 32 * slot - 27)) for slot, row in enumerate((upper, lower, lower, upper))]
    return jnp.pad(jnp.stack(rows), ((0, MASK_ROWS - 4), (0, 0)))


def near_valid(row_valid):
    padded = jnp.pad(row_valid, ((TF, TF), (4, 4)))
    near = lax.dynamic_slice(padded, (lax.axis_index("tm") * TF, lax.axis_index("row") * 4), (3 * TF, 12))
    flat = jnp.pad(near.reshape(1, 72), ((0, 0), (0, 56)))
    return jnp.broadcast_to(flat, (16, 128)).astype(jnp.bfloat16)


def whole():
    return pl.BlockSpec(memory_space=pltpu.VMEM)


def shards(queries, key_states, value_states, grad_output, window_mask, row_valid):
    features = queries.shape[3]
    query, key, value, grad = (x.reshape(OWN, features) for x in (queries, key_states, value_states, grad_output))
    valid = near_valid(row_valid)
    picks = [jnp.asarray(x, jnp.bfloat16) for x in selectors()]
    parts = []
    for first, heads in GROUPS:
        lanes = slice(first * HD, (first + heads) * HD)
        width = heads * HD
        pair = jnp.concatenate([key[:, lanes], value[:, lanes]])
        low, high = shifted(pair, "tm", 1), shifted(pair, "tm", -1)
        message = jnp.concatenate(
            [low[:OWN], key[:, lanes], high[:OWN], low[OWN:], value[:, lanes], high[OWN:]]
            + [query[:, lanes], grad[:, lanes], mask_block(window_mask, width)]
        )
        above, below = shifted(message, "row", 1), shifted(message, "row", -1)
        output, grad_query, own_sum, low_sum, high_sum = pl.pallas_call(
            functools.partial(attend, heads),
            out_shape=(
                jax.ShapeDtypeStruct((OWN, width), jnp.bfloat16),
                jax.ShapeDtypeStruct((OWN, width), jnp.bfloat16),
                jax.ShapeDtypeStruct((2 * OWN, width), jnp.float32),
                jax.ShapeDtypeStruct((2 * OWN, width), jnp.bfloat16),
                jax.ShapeDtypeStruct((2 * OWN, width), jnp.bfloat16),
            ),
            in_specs=[whole()] * 7,
            out_specs=(whole(),) * 5,
            compiler_params=pltpu.CompilerParams(vmem_limit_bytes=40 * 1024 * 1024),
            cost_estimate=pl.CostEstimate(flops=heads * 400_000_000, bytes_accessed=8_000_000, transcendentals=0),
        )(message, above, below, valid, *picks)
        total = own_sum + shifted(low_sum, "tm", -1).astype(jnp.float32) + shifted(high_sum, "tm", 1).astype(jnp.float32)
        parts.append((output, grad_query, total[:OWN].astype(jnp.bfloat16), total[OWN:].astype(jnp.bfloat16)))
    return tuple(jnp.concatenate(pieces, axis=1).reshape(queries.shape) for pieces in zip(*parts))


def solution(mesh):
    placed = P("tm", "row", None, "head")
    return jax.shard_map(
        shards,
        mesh=mesh,
        in_specs=(placed, placed, placed, placed, P("tm", "row", None, None), P()),
        out_specs=(placed,) * 4,
        check_vma=False,
    )
```

```python
import functools
import math

import jax
import jax.numpy as jnp
from jax import lax
from jax.experimental import pallas as pl
from jax.experimental.pallas import tpu as pltpu
from jax.sharding import PartitionSpec as P

HD = 128
TF = 2
BAND = 64
HALF = BAND // 2
OWN = TF * BAND
TILE = TF * HALF
NEAR = 3 * OWN
MASK_ROWS = 16
GROUPS = ((0, 5),)
LATE = 2

SCALE = HD ** (-0.5)
SCALE_LOG2 = SCALE * math.log2(math.e)
FAR = 1e30


def contract(left, right, dims):
    return lax.dot_general(left, right, ((dims[:1], dims[1:]), ((), ())), preferred_element_type=jnp.float32)


SLOT_TILE = (2, 3, 1, 4)


def other_tile(slot, half):
    return ((1, 4), (1, 4), (0, 1), (4, 5))[slot][half]


def lane_facts(lanes):
    lane = lax.broadcasted_iota(jnp.int32, (1, lanes), 1)
    return lane // BAND, lane % BAND // HALF, lane % HALF // 16


def mask_places():
    frame, half, _ = lane_facts(NEAR)
    blocks = []
    for slot in range(4):
        at = []
        for tile in (2 + half, jnp.where(half == 0, other_tile(slot, 0), other_tile(slot, 1))):
            step = tile - SLOT_TILE[slot]
            at.append(jnp.where(jnp.abs(step) <= 1, 9 * (frame // TF) + 3 * (step + 1) + 1, -1))
        at = jnp.concatenate(at, axis=1)
        entry = lax.broadcasted_iota(jnp.int32, (32, 2 * NEAR), 0)
        blocks.append((entry == at).astype(jnp.float32))
    return jnp.concatenate(blocks).astype(jnp.bfloat16)


def live_keys(row_valid, first_frame, first_row):
    frame, half, row = lane_facts(NEAR)
    rows = [4 + 2 * half + row]
    rows += [2 * jnp.where(half == 0, other_tile(slot, 0), other_tile(slot, 1)) + row for slot in (0, 2, 3)]
    rows = jnp.concatenate(rows, axis=1) + first_row
    frames = jnp.concatenate([frame] * 4, axis=1) + first_frame
    count, here = row_valid.shape
    pick = (lax.broadcasted_iota(jnp.int32, (here, 4 * NEAR), 0) == rows).astype(jnp.float32)
    found = contract(row_valid, pick, (1, 0))
    return jnp.sum(jnp.where(lax.broadcasted_iota(jnp.int32, (count, 4 * NEAR), 0) == frames, found, 0.0), axis=0, keepdims=True)


def live_queries(row_valid, first_frame, first_row):
    count, here = row_valid.shape
    token = lax.broadcasted_iota(jnp.int32, (4 * TILE, 1), 0)
    slot = token // TILE
    tile = jnp.where(slot < 2, slot + 2, jnp.where(slot == 2, 1, 4))
    frames = first_frame + TF + token % TILE // HALF
    rows = first_row + 2 * tile + token % HALF // 16
    pick = (lax.broadcasted_iota(jnp.int32, (4 * TILE, here), 1) == rows).astype(jnp.float32)
    found = contract(pick, row_valid, (1, 1))
    return jnp.sum(jnp.where(lax.broadcasted_iota(jnp.int32, (4 * TILE, count), 1) == frames, found, 0.0), axis=1, keepdims=True)


def row_tile(block, half):
    return jnp.concatenate([block[f * BAND + half * HALF : f * BAND + (half + 1) * HALF] for f in range(TF)])


def beside(above, below):
    parts = []
    for start in range(0, NEAR, BAND):
        parts += [above[start + HALF : start + BAND], below[start : start + HALF]]
    return jnp.concatenate(parts)


def store_tiles(ref, value, lanes):
    for half in range(2):
        for frame in range(TF):
            start = frame * BAND + half * HALF
            source = half * TILE + frame * HALF
            ref[start : start + HALF, lanes] = value[source : source + HALF]


def attend(heads, first, *refs):
    (query_ref, key_ref, value_ref, grad_ref, low, high, above, below), refs = refs[:8], refs[8:]
    far_above, far_below, refs = refs[:LATE], refs[LATE : 2 * LATE], refs[2 * LATE :]
    (window_mask, row_valid), refs = refs[:2], refs[2:]
    output, grad_query, own_sum, low_sum, high_sum, held = refs

    mask_at = 2 * OWN + 2 * TILE
    here, up, down = (
        block.astype(jnp.float32)
        for block in (
            padded_masks(window_mask, held),
            above[mask_at : mask_at + MASK_ROWS, :128],
            below[mask_at : mask_at + MASK_ROWS, :128],
        )
    )
    sources = (here[0:1], here[1:2], up[1:2], down[0:1])
    slot = lax.broadcasted_iota(jnp.int32, (MASK_ROWS, 128), 0)
    masks = jnp.zeros((MASK_ROWS, 128), jnp.float32)
    for index, source in enumerate(sources):
        row = jnp.broadcast_to(source, (MASK_ROWS, 128))
        masks = jnp.where(slot == index, pltpu.roll(row, 32 * index, 1), masks)
    kept = contract(masks.astype(jnp.bfloat16), mask_places(), (1, 0))
    first_frame = (lax.axis_index("tm") - 1) * TF
    first_row = (lax.axis_index("row") - 1) * 4
    row_valid = row_valid[...].astype(jnp.float32)
    live = live_keys(row_valid, first_frame, first_row)
    query_live = live_queries(row_valid, first_frame, first_row)
    bias_own, bias_other = [], []
    for index in range(4):
        part = max(index - 1, 0) + 1
        keep_own = kept[index : index + 1, :NEAR] * live[:1, :NEAR]
        keep_other = kept[index : index + 1, NEAR:] * live[:1, part * NEAR : (part + 1) * NEAR]
        bias_own.append(jnp.broadcast_to((keep_own - 1.0) * FAR, (TILE, NEAR)))
        bias_other.append(jnp.broadcast_to((keep_other - 1.0) * FAR, (TILE, NEAR)))
    bias_own = jnp.concatenate(bias_own)
    bias_other = jnp.concatenate(bias_other)

    def far(refs, side, part, lanes):
        ref = refs[side % LATE]
        start = (side * 2 * OWN if LATE == 1 else 0) + part * OWN
        return ref[start : start + OWN, lanes]

    for head in range(heads):
        lanes = slice(head * HD, (head + 1) * HD)
        arg_lanes = slice((first + head) * HD, (first + head + 1) * HD)
        query_own, grad_own = query_ref[:, arg_lanes], grad_ref[:, arg_lanes]
        at = 2 * OWN
        query = jnp.concatenate(
            [row_tile(query_own, 0), row_tile(query_own, 1), above[at : at + TILE, lanes], below[at : at + TILE, lanes]]
        )
        at += TILE
        grad = jnp.concatenate(
            [row_tile(grad_own, 0), row_tile(grad_own, 1), above[at : at + TILE, lanes], below[at : at + TILE, lanes]]
        )

        def region(part, ref):
            rows = slice(part * OWN, (part + 1) * OWN)
            here = jnp.concatenate([low[rows, lanes], ref[:, arg_lanes], high[rows, lanes]])
            up = jnp.concatenate([far(far_above, 0, part, lanes), above[rows, lanes], far(far_above, 1, part, lanes)])
            down = jnp.concatenate([far(far_below, 0, part, lanes), below[rows, lanes], far(far_below, 1, part, lanes)])
            return here, up, down, beside(up, down)

        key_own, key_up, key_down, key_side = region(0, key_ref)
        value_own, value_up, value_down, value_side = region(1, value_ref)

        score_own = contract(query, key_own, (1, 1)) * SCALE_LOG2 + bias_own
        score_other = (
            jnp.concatenate(
                [
                    contract(query[:OWN], key_side, (1, 1)),
                    contract(query[OWN : OWN + TILE], key_up, (1, 1)),
                    contract(query[OWN + TILE :], key_down, (1, 1)),
                ]
            )
            * SCALE_LOG2
            + bias_other
        )
        row_max = jnp.max(jnp.maximum(score_own, score_other), axis=1, keepdims=True)
        own = jnp.exp2(score_own - row_max)
        other = jnp.exp2(score_other - row_max)
        share = query_live / jnp.sum(own + other, axis=1, keepdims=True)
        own_bf, other_bf = own.astype(jnp.bfloat16), other.astype(jnp.bfloat16)
        attended = contract(own_bf, value_own, (1, 0)) + jnp.concatenate(
            [
                contract(other_bf[:OWN], value_side, (1, 0)),
                contract(other_bf[OWN : OWN + TILE], value_up, (1, 0)),
                contract(other_bf[OWN + TILE :], value_down, (1, 0)),
            ]
        )
        result = (attended * share).astype(jnp.bfloat16)
        row_dot = jnp.sum(result.astype(jnp.float32) * grad.astype(jnp.float32), axis=1, keepdims=True)
        weight_own = own * share
        weight_side = other[:OWN] * share[:OWN]
        grad_score_own = (weight_own * (contract(grad, value_own, (1, 1)) - row_dot)).astype(jnp.bfloat16)
        grad_score_side = (weight_side * (contract(grad[:OWN], value_side, (1, 1)) - row_dot[:OWN])).astype(jnp.bfloat16)
        query_sum = contract(grad_score_own[:OWN], key_own, (1, 0)) + contract(grad_score_side, key_side, (1, 0))
        key_sum = contract(grad_score_own, query, (0, 0)) * SCALE
        value_sum = contract(weight_own.astype(jnp.bfloat16), grad, (0, 0))

        store_tiles(output, result, lanes)
        store_tiles(grad_query, (query_sum * SCALE).astype(jnp.bfloat16), lanes)
        for part, total in enumerate((key_sum, value_sum)):
            rows = slice(part * OWN, (part + 1) * OWN)
            low_sum[rows, lanes] = total[:OWN].astype(jnp.bfloat16)
            own_sum[rows, lanes] = total[OWN : 2 * OWN]
            high_sum[rows, lanes] = total[2 * OWN :].astype(jnp.bfloat16)


def shifted(value, axis, steps):
    count = lax.axis_size(axis)
    leading, last = (max(0, -steps), min(count, count - steps))
    return lax.ppermute(value, axis, [(source, source + steps) for source in range(leading, last)])


def ring(value, axis, steps):
    count = lax.axis_size(axis)
    return lax.ppermute(value, axis, [(source, (source + steps) % count) for source in range(count)])


def padded_masks(window_mask, held):
    held[...] = jnp.zeros_like(held)
    for tile in range(2):
        held[tile : tile + 1, :27] = window_mask[0, tile].astype(jnp.float32)
    return held[...]


def pack(first, heads, query, key, value, grad, window_mask, pair, near_up, near_down, stage, held, block, sems):
    lanes = slice(first * HD, (first + heads) * HD)
    loads, copies = [], []
    for part, ref in enumerate((key, value, query, grad)):
        loads.append(pltpu.make_async_copy(ref.at[:, lanes], stage.at[part], sems.at[part]))
        loads[-1].start()

    def copy(source, target):
        copies.append(pltpu.make_async_copy(source, target, sems.at[4 + len(copies)]))
        copies[-1].start()

    block[...] = padded_masks(window_mask, held).astype(jnp.bfloat16)
    rows = slice(2 * OWN + 2 * TILE, 2 * OWN + 2 * TILE + MASK_ROWS)
    for target in (near_up, near_down):
        copy(block, target.at[rows, :128])
    for part in range(2):
        loads[part].wait()
        rows = slice(part * OWN, (part + 1) * OWN)
        for target in (pair, near_up, near_down):
            copy(stage.at[part], target.at[rows])
    for part in range(2):
        loads[2 + part].wait()
        for half, target in enumerate((near_down, near_up)):
            for frame in range(TF):
                at = 2 * OWN + part * TILE + frame * HALF
                start = frame * BAND + half * HALF
                copy(stage.at[2 + part, start : start + HALF], target.at[at : at + HALF])
    for started in copies:
        started.wait()


def whole():
    return pl.BlockSpec(memory_space=pltpu.VMEM)


def shards(queries, key_states, value_states, grad_output, window_mask, row_valid):
    features = queries.shape[3]
    query, key, value, grad = (x.reshape(OWN, features) for x in (queries, key_states, value_states, grad_output))
    parts = []
    for first, heads in GROUPS:
        width = heads * HD
        pair, near_up, near_down = pl.pallas_call(
            functools.partial(pack, first, heads),
            out_shape=[
                jax.ShapeDtypeStruct((rows, width), jnp.bfloat16)
                for rows in (2 * OWN, *[2 * OWN + 2 * TILE + MASK_ROWS] * 2)
            ],
            in_specs=[pl.BlockSpec(memory_space=pl.ANY)] * 4 + [whole()],
            out_specs=[pl.BlockSpec(memory_space=pl.ANY)] * 3,
            scratch_shapes=[
                pltpu.VMEM((4, OWN, width), jnp.bfloat16),
                pltpu.VMEM((MASK_ROWS, 128), jnp.float32),
                pltpu.VMEM((MASK_ROWS, 128), jnp.bfloat16),
                pltpu.SemaphoreType.DMA((20,)),
            ],
            cost_estimate=pl.CostEstimate(flops=0, bytes_accessed=2_000_000, transcendentals=0),
        )(query, key, value, grad, window_mask)
        low, high = shifted(pair, "tm", 1), shifted(pair, "tm", -1)
        above, below = ring(near_up, "row", 1), ring(near_down, "row", -1)
        far = [jnp.concatenate([low, high])] if LATE == 1 else [low, high]
        far_above = [ring(x, "row", 1) for x in far]
        far_below = [ring(x, "row", -1) for x in far]
        output, grad_query, own_sum, low_sum, high_sum = pl.pallas_call(
            functools.partial(attend, heads, first),
            out_shape=(
                jax.ShapeDtypeStruct((OWN, width), jnp.bfloat16),
                jax.ShapeDtypeStruct((OWN, width), jnp.bfloat16),
                jax.ShapeDtypeStruct((2 * OWN, width), jnp.float32),
                jax.ShapeDtypeStruct((2 * OWN, width), jnp.bfloat16),
                jax.ShapeDtypeStruct((2 * OWN, width), jnp.bfloat16),
            ),
            in_specs=[whole()] * (10 + 2 * LATE),
            out_specs=(whole(),) * 5,
            scratch_shapes=[pltpu.VMEM((MASK_ROWS, 128), jnp.float32)],
            compiler_params=pltpu.CompilerParams(vmem_limit_bytes=40 * 1024 * 1024),
            cost_estimate=pl.CostEstimate(flops=heads * 400_000_000, bytes_accessed=8_000_000, transcendentals=0),
        )(query, key, value, grad, low, high, above, below, *far_above, *far_below, window_mask, row_valid)
        total = own_sum + shifted(low_sum, "tm", -1).astype(jnp.float32) + shifted(high_sum, "tm", 1).astype(jnp.float32)
        parts.append((output, grad_query, total[:OWN].astype(jnp.bfloat16), total[OWN:].astype(jnp.bfloat16)))
    return tuple(jnp.concatenate(pieces, axis=1).reshape(queries.shape) for pieces in zip(*parts))


def solution(mesh):
    placed = P("tm", "row", None, "head")
    return jax.shard_map(
        shards,
        mesh=mesh,
        in_specs=(placed, placed, placed, placed, P("tm", "row", None, None), P()),
        out_specs=(placed,) * 4,
        check_vma=False,
    )
```

```python
import functools
import math

import jax
import jax.numpy as jnp
from jax import lax
from jax.experimental import pallas as pl
from jax.experimental.pallas import tpu as pltpu
from jax.sharding import PartitionSpec as P

HD = 128
TF = 2
BAND = 64
HALF = BAND // 2
OWN = TF * BAND
TILE = TF * HALF
NEAR = 3 * OWN
MASK_ROWS = 16
GROUPS = ((0, 5),)
LATE = 2

SCALE = HD ** (-0.5)
SCALE_LOG2 = SCALE * math.log2(math.e)
FAR = 1e30


def contract(left, right, dims):
    return lax.dot_general(left, right, ((dims[:1], dims[1:]), ((), ())), preferred_element_type=jnp.float32)


SLOT_TILE = (2, 3, 1, 4)


def other_tile(slot, half):
    return ((1, 4), (1, 4), (0, 1), (4, 5))[slot][half]


def lane_facts(lanes):
    lane = lax.broadcasted_iota(jnp.int32, (1, lanes), 1)
    return lane // BAND, lane % BAND // HALF, lane % HALF // 16


def mask_places():
    frame, half, _ = lane_facts(NEAR)
    blocks = []
    for slot in range(4):
        at = []
        for tile in (2 + half, jnp.where(half == 0, other_tile(slot, 0), other_tile(slot, 1))):
            step = tile - SLOT_TILE[slot]
            at.append(jnp.where(jnp.abs(step) <= 1, 9 * (frame // TF) + 3 * (step + 1) + 1, -1))
        at = jnp.concatenate(at, axis=1)
        entry = lax.broadcasted_iota(jnp.int32, (32, 2 * NEAR), 0)
        blocks.append((entry == at).astype(jnp.float32))
    return jnp.concatenate(blocks).astype(jnp.bfloat16)


def live_keys(row_valid, first_frame, first_row):
    frame, half, row = lane_facts(NEAR)
    rows = [4 + 2 * half + row]
    rows += [2 * jnp.where(half == 0, other_tile(slot, 0), other_tile(slot, 1)) + row for slot in (0, 2, 3)]
    rows = jnp.concatenate(rows, axis=1) + first_row
    frames = jnp.concatenate([frame] * 4, axis=1) + first_frame
    count, here = row_valid.shape
    pick = (lax.broadcasted_iota(jnp.int32, (here, 4 * NEAR), 0) == rows).astype(jnp.float32)
    found = contract(row_valid, pick, (1, 0))
    return jnp.sum(jnp.where(lax.broadcasted_iota(jnp.int32, (count, 4 * NEAR), 0) == frames, found, 0.0), axis=0, keepdims=True)


def live_queries(row_valid, first_frame, first_row):
    count, here = row_valid.shape
    token = lax.broadcasted_iota(jnp.int32, (4 * TILE, 1), 0)
    slot = token // TILE
    tile = jnp.where(slot < 2, slot + 2, jnp.where(slot == 2, 1, 4))
    frames = first_frame + TF + token % TILE // HALF
    rows = first_row + 2 * tile + token % HALF // 16
    pick = (lax.broadcasted_iota(jnp.int32, (4 * TILE, here), 1) == rows).astype(jnp.float32)
    found = contract(pick, row_valid, (1, 1))
    return jnp.sum(jnp.where(lax.broadcasted_iota(jnp.int32, (4 * TILE, count), 1) == frames, found, 0.0), axis=1, keepdims=True)


def row_tile(block, half):
    return jnp.concatenate([block[f * BAND + half * HALF : f * BAND + (half + 1) * HALF] for f in range(TF)])


def beside(above, below):
    parts = []
    for start in range(0, NEAR, BAND):
        parts += [above[start + HALF : start + BAND], below[start : start + HALF]]
    return jnp.concatenate(parts)


def store_tiles(ref, value, lanes):
    for half in range(2):
        for frame in range(TF):
            start = frame * BAND + half * HALF
            source = half * TILE + frame * HALF
            ref[start : start + HALF, lanes] = value[source : source + HALF]


def attend(heads, first, *refs):
    (query_ref, key_ref, value_ref, grad_ref, low, high, above, below), refs = refs[:8], refs[8:]
    far_above, far_below, refs = refs[:LATE], refs[LATE : 2 * LATE], refs[2 * LATE :]
    (window_mask, row_valid), refs = refs[:2], refs[2:]
    output, grad_query, own_sum, low_sum, high_sum, held = refs

    mask_at = 2 * OWN + 2 * TILE
    here, up, down = (
        block.astype(jnp.float32)
        for block in (
            padded_masks(window_mask, held),
            above[mask_at : mask_at + MASK_ROWS, :128],
            below[mask_at : mask_at + MASK_ROWS, :128],
        )
    )
    sources = (here[0:1], here[1:2], up[1:2], down[0:1])
    slot = lax.broadcasted_iota(jnp.int32, (MASK_ROWS, 128), 0)
    masks = jnp.zeros((MASK_ROWS, 128), jnp.float32)
    for index, source in enumerate(sources):
        row = jnp.broadcast_to(source, (MASK_ROWS, 128))
        masks = jnp.where(slot == index, pltpu.roll(row, 32 * index, 1), masks)
    kept = contract(masks.astype(jnp.bfloat16), mask_places(), (1, 0))
    first_frame = (lax.axis_index("tm") - 1) * TF
    first_row = (lax.axis_index("row") - 1) * 4
    row_valid = row_valid[...].astype(jnp.float32)
    live = live_keys(row_valid, first_frame, first_row)
    query_live = live_queries(row_valid, first_frame, first_row)
    bias_own, bias_other = [], []
    for index in range(4):
        part = max(index - 1, 0) + 1
        keep_own = kept[index : index + 1, :NEAR] * live[:1, :NEAR]
        keep_other = kept[index : index + 1, NEAR:] * live[:1, part * NEAR : (part + 1) * NEAR]
        bias_own.append(jnp.broadcast_to((keep_own - 1.0) * FAR, (TILE, NEAR)))
        bias_other.append(jnp.broadcast_to((keep_other - 1.0) * FAR, (TILE, NEAR)))
    bias_own = jnp.concatenate(bias_own)
    bias_other = jnp.concatenate(bias_other)

    def far(refs, side, part, lanes):
        ref = refs[side % LATE]
        start = (side * 2 * OWN if LATE == 1 else 0) + part * OWN
        return ref[start : start + OWN, lanes]

    for head in range(heads):
        lanes = slice(head * HD, (head + 1) * HD)
        arg_lanes = slice((first + head) * HD, (first + head + 1) * HD)
        query_own, grad_own = query_ref[:, arg_lanes], grad_ref[:, arg_lanes]
        at = 2 * OWN
        query = jnp.concatenate(
            [row_tile(query_own, 0), row_tile(query_own, 1), above[at : at + TILE, lanes], below[at : at + TILE, lanes]]
        )
        at += TILE
        grad = jnp.concatenate(
            [row_tile(grad_own, 0), row_tile(grad_own, 1), above[at : at + TILE, lanes], below[at : at + TILE, lanes]]
        )

        def region(part, ref):
            rows = slice(part * OWN, (part + 1) * OWN)
            here = jnp.concatenate([low[rows, lanes], ref[:, arg_lanes], high[rows, lanes]])
            up = jnp.concatenate([far(far_above, 0, part, lanes), above[rows, lanes], far(far_above, 1, part, lanes)])
            down = jnp.concatenate([far(far_below, 0, part, lanes), below[rows, lanes], far(far_below, 1, part, lanes)])
            return here, up, down, beside(up, down)

        key_own, key_up, key_down, key_side = region(0, key_ref)
        value_own, value_up, value_down, value_side = region(1, value_ref)

        score_own = contract(query, key_own, (1, 1)) * SCALE_LOG2 + bias_own
        score_other = (
            jnp.concatenate(
                [
                    contract(query[:OWN], key_side, (1, 1)),
                    contract(query[OWN : OWN + TILE], key_up, (1, 1)),
                    contract(query[OWN + TILE :], key_down, (1, 1)),
                ]
            )
            * SCALE_LOG2
            + bias_other
        )
        row_max = jnp.max(jnp.maximum(score_own, score_other), axis=1, keepdims=True)
        own = jnp.exp2(score_own - row_max)
        other = jnp.exp2(score_other - row_max)
        share = query_live / jnp.sum(own + other, axis=1, keepdims=True)
        own_bf, other_bf = own.astype(jnp.bfloat16), other.astype(jnp.bfloat16)
        attended = contract(own_bf, value_own, (1, 0)) + jnp.concatenate(
            [
                contract(other_bf[:OWN], value_side, (1, 0)),
                contract(other_bf[OWN : OWN + TILE], value_up, (1, 0)),
                contract(other_bf[OWN + TILE :], value_down, (1, 0)),
            ]
        )
        result = (attended * share).astype(jnp.bfloat16)
        row_dot = jnp.sum(result.astype(jnp.float32) * grad.astype(jnp.float32), axis=1, keepdims=True)
        weight_own = own * share
        weight_side = other[:OWN] * share[:OWN]
        grad_score_own = (weight_own * (contract(grad, value_own, (1, 1)) - row_dot)).astype(jnp.bfloat16)
        grad_score_side = (weight_side * (contract(grad[:OWN], value_side, (1, 1)) - row_dot[:OWN])).astype(jnp.bfloat16)
        query_sum = contract(grad_score_own[:OWN], key_own, (1, 0)) + contract(grad_score_side, key_side, (1, 0))
        key_sum = contract(grad_score_own, query, (0, 0)) * SCALE
        value_sum = contract(weight_own.astype(jnp.bfloat16), grad, (0, 0))

        store_tiles(output, result, lanes)
        store_tiles(grad_query, (query_sum * SCALE).astype(jnp.bfloat16), lanes)
        for part, total in enumerate((key_sum, value_sum)):
            rows = slice(part * OWN, (part + 1) * OWN)
            low_sum[rows, lanes] = total[:OWN].astype(jnp.bfloat16)
            own_sum[rows, lanes] = total[OWN : 2 * OWN]
            high_sum[rows, lanes] = total[2 * OWN :].astype(jnp.bfloat16)


def shifted(value, axis, steps):
    count = lax.axis_size(axis)
    leading, last = (max(0, -steps), min(count, count - steps))
    return lax.ppermute(value, axis, [(source, source + steps) for source in range(leading, last)])


def ring(value, axis, steps):
    count = lax.axis_size(axis)
    return lax.ppermute(value, axis, [(source, (source + steps) % count) for source in range(count)])


def padded_masks(window_mask, held):
    held[...] = jnp.zeros_like(held)
    for tile in range(2):
        held[tile : tile + 1, :27] = window_mask[0, tile].astype(jnp.float32)
    return held[...]


def pack(first, heads, query, key, value, grad, window_mask, pair, near_up, near_down, held):
    lanes = slice(first * HD, (first + heads) * HD)
    for part, ref in enumerate((key, value)):
        rows = slice(part * OWN, (part + 1) * OWN)
        block = ref[:, lanes]
        for target in (pair, near_up, near_down):
            target[rows] = block
    for part, ref in enumerate((query, grad)):
        rows = slice(2 * OWN + part * TILE, 2 * OWN + (part + 1) * TILE)
        block = ref[:, lanes]
        near_down[rows] = row_tile(block, 0)
        near_up[rows] = row_tile(block, 1)
    masks = padded_masks(window_mask, held).astype(jnp.bfloat16)
    rows = slice(2 * OWN + 2 * TILE, 2 * OWN + 2 * TILE + MASK_ROWS)
    for target in (near_up, near_down):
        target[rows] = jnp.zeros((MASK_ROWS, heads * HD), jnp.bfloat16)
        target[rows, :128] = masks


def whole():
    return pl.BlockSpec(memory_space=pltpu.VMEM)


def shards(queries, key_states, value_states, grad_output, window_mask, row_valid):
    features = queries.shape[3]
    query, key, value, grad = (x.reshape(OWN, features) for x in (queries, key_states, value_states, grad_output))
    parts = []
    for first, heads in GROUPS:
        width = heads * HD
        pair, near_up, near_down = pl.pallas_call(
            functools.partial(pack, first, heads),
            out_shape=[
                jax.ShapeDtypeStruct((rows, width), jnp.bfloat16)
                for rows in (2 * OWN, *[2 * OWN + 2 * TILE + MASK_ROWS] * 2)
            ],
            in_specs=[whole()] * 5,
            out_specs=[whole()] * 3,
            scratch_shapes=[pltpu.VMEM((MASK_ROWS, 128), jnp.float32)],
            cost_estimate=pl.CostEstimate(flops=0, bytes_accessed=2_000_000, transcendentals=0),
        )(query, key, value, grad, window_mask)
        low, high = shifted(pair, "tm", 1), shifted(pair, "tm", -1)
        above, below = ring(near_up, "row", 1), ring(near_down, "row", -1)
        far = [low, high]
        far_above = [ring(x, "row", 1) for x in far]
        far_below = [ring(x, "row", -1) for x in far]
        output, grad_query, own_sum, low_sum, high_sum = pl.pallas_call(
            functools.partial(attend, heads, first),
            out_shape=(
                jax.ShapeDtypeStruct((OWN, width), jnp.bfloat16),
                jax.ShapeDtypeStruct((OWN, width), jnp.bfloat16),
                jax.ShapeDtypeStruct((2 * OWN, width), jnp.float32),
                jax.ShapeDtypeStruct((2 * OWN, width), jnp.bfloat16),
                jax.ShapeDtypeStruct((2 * OWN, width), jnp.bfloat16),
            ),
            in_specs=[whole()] * (10 + 2 * LATE),
            out_specs=(whole(),) * 5,
            scratch_shapes=[pltpu.VMEM((MASK_ROWS, 128), jnp.float32)],
            compiler_params=pltpu.CompilerParams(vmem_limit_bytes=40 * 1024 * 1024),
            cost_estimate=pl.CostEstimate(flops=heads * 400_000_000, bytes_accessed=8_000_000, transcendentals=0),
        )(query, key, value, grad, low, high, above, below, *far_above, *far_below, window_mask, row_valid)
        total = own_sum + shifted(low_sum, "tm", -1).astype(jnp.float32) + shifted(high_sum, "tm", 1).astype(jnp.float32)
        parts.append((output, grad_query, total[:OWN].astype(jnp.bfloat16), total[OWN:].astype(jnp.bfloat16)))
    return tuple(jnp.concatenate(pieces, axis=1).reshape(queries.shape) for pieces in zip(*parts))


def solution(mesh):
    placed = P("tm", "row", None, "head")
    return jax.shard_map(
        shards,
        mesh=mesh,
        in_specs=(placed, placed, placed, placed, P("tm", "row", None, None), P()),
        out_specs=(placed,) * 4,
        check_vma=False,
    )
```

```python
import functools
import math

import jax
import jax.numpy as jnp
from jax import lax
from jax.experimental import pallas as pl
from jax.experimental.pallas import tpu as pltpu
from jax.sharding import PartitionSpec as P

HD = 128
TF = 2
BAND = 64
HALF = BAND // 2
OWN = TF * BAND
TILE = TF * HALF
NEAR = 3 * OWN
MASK_ROWS = 16
GROUPS = ((0, 5),)
LATE = 2

SCALE = HD ** (-0.5)
SCALE_LOG2 = SCALE * math.log2(math.e)
FAR = 1e30


def contract(left, right, dims):
    return lax.dot_general(left, right, ((dims[:1], dims[1:]), ((), ())), preferred_element_type=jnp.float32)


SLOT_TILE = (2, 3, 1, 4)


def other_tile(slot, half):
    return ((1, 4), (1, 4), (0, 1), (4, 5))[slot][half]


def lane_facts(lanes):
    lane = lax.broadcasted_iota(jnp.int32, (1, lanes), 1)
    return lane // BAND, lane % BAND // HALF, lane % HALF // 16


def mask_places():
    frame, half, _ = lane_facts(NEAR)
    blocks = []
    for slot in range(4):
        at = []
        for tile in (2 + half, jnp.where(half == 0, other_tile(slot, 0), other_tile(slot, 1))):
            step = tile - SLOT_TILE[slot]
            at.append(jnp.where(jnp.abs(step) <= 1, 9 * (frame // TF) + 3 * (step + 1) + 1, -1))
        at = jnp.concatenate(at, axis=1)
        entry = lax.broadcasted_iota(jnp.int32, (32, 2 * NEAR), 0)
        blocks.append((entry == at).astype(jnp.float32))
    return jnp.concatenate(blocks).astype(jnp.bfloat16)


def live_keys(row_valid, first_frame, first_row):
    frame, half, row = lane_facts(NEAR)
    rows = [4 + 2 * half + row]
    rows += [2 * jnp.where(half == 0, other_tile(slot, 0), other_tile(slot, 1)) + row for slot in (0, 2, 3)]
    rows = jnp.concatenate(rows, axis=1) + first_row
    frames = jnp.concatenate([frame] * 4, axis=1) + first_frame
    count, here = row_valid.shape
    pick = (lax.broadcasted_iota(jnp.int32, (here, 4 * NEAR), 0) == rows).astype(jnp.float32)
    found = contract(row_valid, pick, (1, 0))
    return jnp.sum(jnp.where(lax.broadcasted_iota(jnp.int32, (count, 4 * NEAR), 0) == frames, found, 0.0), axis=0, keepdims=True)


def live_queries(row_valid, first_frame, first_row):
    count, here = row_valid.shape
    token = lax.broadcasted_iota(jnp.int32, (4 * TILE, 1), 0)
    slot = token // TILE
    tile = jnp.where(slot < 2, slot + 2, jnp.where(slot == 2, 1, 4))
    frames = first_frame + TF + token % TILE // HALF
    rows = first_row + 2 * tile + token % HALF // 16
    pick = (lax.broadcasted_iota(jnp.int32, (4 * TILE, here), 1) == rows).astype(jnp.float32)
    found = contract(pick, row_valid, (1, 1))
    return jnp.sum(jnp.where(lax.broadcasted_iota(jnp.int32, (4 * TILE, count), 1) == frames, found, 0.0), axis=1, keepdims=True)


def row_tile(block, half):
    return jnp.concatenate([block[f * BAND + half * HALF : f * BAND + (half + 1) * HALF] for f in range(TF)])


def beside(above, below):
    parts = []
    for start in range(0, NEAR, BAND):
        parts += [above[start + HALF : start + BAND], below[start : start + HALF]]
    return jnp.concatenate(parts)


def store_tiles(ref, value, lanes):
    for half in range(2):
        for frame in range(TF):
            start = frame * BAND + half * HALF
            source = half * TILE + frame * HALF
            ref[start : start + HALF, lanes] = value[source : source + HALF]


def attend(heads, first, *refs):
    (query_ref, key_ref, value_ref, grad_ref, low, high, above, below, query_above, query_below), refs = refs[:10], refs[10:]
    far_above, far_below, refs = refs[:LATE], refs[LATE : 2 * LATE], refs[2 * LATE :]
    (window_mask, row_valid), refs = refs[:2], refs[2:]
    output, grad_query, own_sum, low_sum, high_sum, held = refs

    mask_at = 2 * TILE
    here, up, down = (
        block.astype(jnp.float32)
        for block in (
            padded_masks(window_mask, held),
            query_above[mask_at : mask_at + MASK_ROWS, :128],
            query_below[mask_at : mask_at + MASK_ROWS, :128],
        )
    )
    sources = (here[0:1], here[1:2], up[1:2], down[0:1])
    slot = lax.broadcasted_iota(jnp.int32, (MASK_ROWS, 128), 0)
    masks = jnp.zeros((MASK_ROWS, 128), jnp.float32)
    for index, source in enumerate(sources):
        row = jnp.broadcast_to(source, (MASK_ROWS, 128))
        masks = jnp.where(slot == index, pltpu.roll(row, 32 * index, 1), masks)
    kept = contract(masks.astype(jnp.bfloat16), mask_places(), (1, 0))
    first_frame = (lax.axis_index("tm") - 1) * TF
    first_row = (lax.axis_index("row") - 1) * 4
    row_valid = row_valid[...].astype(jnp.float32)
    live = live_keys(row_valid, first_frame, first_row)
    query_live = live_queries(row_valid, first_frame, first_row)
    bias_own, bias_other = [], []
    for index in range(4):
        part = max(index - 1, 0) + 1
        keep_own = kept[index : index + 1, :NEAR] * live[:1, :NEAR]
        keep_other = kept[index : index + 1, NEAR:] * live[:1, part * NEAR : (part + 1) * NEAR]
        bias_own.append(jnp.broadcast_to((keep_own - 1.0) * FAR, (TILE, NEAR)))
        bias_other.append(jnp.broadcast_to((keep_other - 1.0) * FAR, (TILE, NEAR)))
    bias_own = jnp.concatenate(bias_own)
    bias_other = jnp.concatenate(bias_other)

    def far(refs, side, part, lanes):
        ref = refs[side % LATE]
        start = (side * 2 * OWN if LATE == 1 else 0) + part * OWN
        return ref[start : start + OWN, lanes]

    for head in range(heads):
        lanes = slice(head * HD, (head + 1) * HD)
        arg_lanes = slice((first + head) * HD, (first + head + 1) * HD)
        query_own, grad_own = query_ref[:, arg_lanes], grad_ref[:, arg_lanes]
        query = [row_tile(query_own, 0), row_tile(query_own, 1), query_above[:TILE, lanes], query_below[:TILE, lanes]]
        query = jnp.concatenate(query)
        near = slice(TILE, 2 * TILE)
        grad = [row_tile(grad_own, 0), row_tile(grad_own, 1), query_above[near, lanes], query_below[near, lanes]]
        grad = jnp.concatenate(grad)

        def region(part, ref):
            rows = slice(part * OWN, (part + 1) * OWN)
            here = jnp.concatenate([low[rows, lanes], ref[:, arg_lanes], high[rows, lanes]])
            up = jnp.concatenate([far(far_above, 0, part, lanes), above[rows, lanes], far(far_above, 1, part, lanes)])
            down = jnp.concatenate([far(far_below, 0, part, lanes), below[rows, lanes], far(far_below, 1, part, lanes)])
            return here, up, down, beside(up, down)

        key_own, key_up, key_down, key_side = region(0, key_ref)
        value_own, value_up, value_down, value_side = region(1, value_ref)

        score_own = contract(query, key_own, (1, 1)) * SCALE_LOG2 + bias_own
        score_other = (
            jnp.concatenate(
                [
                    contract(query[:OWN], key_side, (1, 1)),
                    contract(query[OWN : OWN + TILE], key_up, (1, 1)),
                    contract(query[OWN + TILE :], key_down, (1, 1)),
                ]
            )
            * SCALE_LOG2
            + bias_other
        )
        row_max = jnp.max(jnp.maximum(score_own, score_other), axis=1, keepdims=True)
        own = jnp.exp2(score_own - row_max)
        other = jnp.exp2(score_other - row_max)
        share = query_live / jnp.sum(own + other, axis=1, keepdims=True)
        own_bf, other_bf = own.astype(jnp.bfloat16), other.astype(jnp.bfloat16)
        attended = contract(own_bf, value_own, (1, 0)) + jnp.concatenate(
            [
                contract(other_bf[:OWN], value_side, (1, 0)),
                contract(other_bf[OWN : OWN + TILE], value_up, (1, 0)),
                contract(other_bf[OWN + TILE :], value_down, (1, 0)),
            ]
        )
        result = (attended * share).astype(jnp.bfloat16)
        row_dot = jnp.sum(result.astype(jnp.float32) * grad.astype(jnp.float32), axis=1, keepdims=True)
        weight_own = own * share
        weight_side = other[:OWN] * share[:OWN]
        grad_score_own = (weight_own * (contract(grad, value_own, (1, 1)) - row_dot)).astype(jnp.bfloat16)
        grad_score_side = (weight_side * (contract(grad[:OWN], value_side, (1, 1)) - row_dot[:OWN])).astype(jnp.bfloat16)
        query_sum = contract(grad_score_own[:OWN], key_own, (1, 0)) + contract(grad_score_side, key_side, (1, 0))
        key_sum = contract(grad_score_own, query, (0, 0)) * SCALE
        value_sum = contract(weight_own.astype(jnp.bfloat16), grad, (0, 0))

        store_tiles(output, result, lanes)
        store_tiles(grad_query, (query_sum * SCALE).astype(jnp.bfloat16), lanes)
        for part, total in enumerate((key_sum, value_sum)):
            rows = slice(part * OWN, (part + 1) * OWN)
            low_sum[rows, lanes] = total[:OWN].astype(jnp.bfloat16)
            own_sum[rows, lanes] = total[OWN : 2 * OWN]
            high_sum[rows, lanes] = total[2 * OWN :].astype(jnp.bfloat16)


def shifted(value, axis, steps):
    count = lax.axis_size(axis)
    leading, last = (max(0, -steps), min(count, count - steps))
    return lax.ppermute(value, axis, [(source, source + steps) for source in range(leading, last)])


def ring(value, axis, steps):
    count = lax.axis_size(axis)
    return lax.ppermute(value, axis, [(source, (source + steps) % count) for source in range(count)])


def padded_masks(window_mask, held):
    held[...] = jnp.zeros_like(held)
    for tile in range(2):
        held[tile : tile + 1, :27] = window_mask[0, tile].astype(jnp.float32)
    return held[...]


def pack(first, heads, query, grad, window_mask, up, down, held):
    lanes = slice(first * HD, (first + heads) * HD)
    masks = padded_masks(window_mask, held).astype(jnp.bfloat16)
    for half, message in enumerate((down, up)):
        message[:TILE] = row_tile(query[:, lanes], half)
        message[TILE : 2 * TILE] = row_tile(grad[:, lanes], half)
        message[2 * TILE :] = jnp.zeros((MASK_ROWS, heads * HD), jnp.bfloat16)
        message[2 * TILE :, :128] = masks


def whole():
    return pl.BlockSpec(memory_space=pltpu.VMEM)


def shards(queries, key_states, value_states, grad_output, window_mask, row_valid):
    features = queries.shape[3]
    query, key, value, grad = (x.reshape(OWN, features) for x in (queries, key_states, value_states, grad_output))
    parts = []
    for first, heads in GROUPS:
        width = heads * HD
        lanes = slice(first * HD, (first + heads) * HD)
        pair = jnp.concatenate([key[:, lanes], value[:, lanes]])
        low, high = shifted(pair, "tm", 1), shifted(pair, "tm", -1)
        above, below = ring(pair, "row", 1), ring(pair, "row", -1)
        up, down = pl.pallas_call(
            functools.partial(pack, first, heads),
            out_shape=[jax.ShapeDtypeStruct((2 * TILE + MASK_ROWS, width), jnp.bfloat16)] * 2,
            in_specs=[whole()] * 3,
            out_specs=[whole()] * 2,
            scratch_shapes=[pltpu.VMEM((MASK_ROWS, 128), jnp.float32)],
            cost_estimate=pl.CostEstimate(flops=0, bytes_accessed=700_000, transcendentals=0),
        )(query, grad, window_mask)
        up, down, high = lax.optimization_barrier((up, down, high))
        query_above, query_below = ring(up, "row", 1), ring(down, "row", -1)
        far = [jnp.concatenate([low, high])] if LATE == 1 else [low, high]
        far_above = [ring(x, "row", 1) for x in far]
        far_below = [ring(x, "row", -1) for x in far]
        output, grad_query, own_sum, low_sum, high_sum = pl.pallas_call(
            functools.partial(attend, heads, first),
            out_shape=(
                jax.ShapeDtypeStruct((OWN, width), jnp.bfloat16),
                jax.ShapeDtypeStruct((OWN, width), jnp.bfloat16),
                jax.ShapeDtypeStruct((2 * OWN, width), jnp.float32),
                jax.ShapeDtypeStruct((2 * OWN, width), jnp.bfloat16),
                jax.ShapeDtypeStruct((2 * OWN, width), jnp.bfloat16),
            ),
            in_specs=[whole()] * (12 + 2 * LATE),
            out_specs=(whole(),) * 5,
            scratch_shapes=[pltpu.VMEM((MASK_ROWS, 128), jnp.float32)],
            compiler_params=pltpu.CompilerParams(vmem_limit_bytes=40 * 1024 * 1024),
            cost_estimate=pl.CostEstimate(flops=heads * 400_000_000, bytes_accessed=8_000_000, transcendentals=0),
        )(query, key, value, grad, low, high, above, below, query_above, query_below, *far_above, *far_below, window_mask, row_valid)
        total = own_sum + shifted(low_sum, "tm", -1).astype(jnp.float32) + shifted(high_sum, "tm", 1).astype(jnp.float32)
        parts.append((output, grad_query, total[:OWN].astype(jnp.bfloat16), total[OWN:].astype(jnp.bfloat16)))
    return tuple(jnp.concatenate(pieces, axis=1).reshape(queries.shape) for pieces in zip(*parts))


def solution(mesh):
    placed = P("tm", "row", None, "head")
    return jax.shard_map(
        shards,
        mesh=mesh,
        in_specs=(placed, placed, placed, placed, P("tm", "row", None, None), P()),
        out_specs=(placed,) * 4,
        check_vma=False,
    )
```
